128 devices in a mesh: grp: 4 (over z), eig: 32 (over y, x, core).
Axes of the slice: x: 4, y: 4, z: 4, core: 2. Of those that a mesh axis runs over, the one named last changes fastest.
Arguments:
- out_grads: bfloat16 [1024, 14336], P(('grp', 'eig')), may hold values from -6 to 6
- activations: bfloat16 [1024, 8192], P(('grp', 'eig')), may hold values from -6 to 6
- grad_basis: bfloat16 [14336, 14336], P(None, 'eig'), may hold values from -0.046875 to 0.046875
- act_basis: bfloat16 [8192, 8192], P(None, 'eig'), may hold values from -0.0625 to 0.0625
- corrections: bfloat16 [14336, 8192], P('eig'), may hold values from 0.049804688 to 5
- query_left: bfloat16 [4, 32, 14336], P(None, None, 'eig'), may hold values from -0.0078125 to 0.0078125
- query_right: bfloat16 [4, 32, 8192], P(None, None, 'eig'), may hold values from -0.0625 to 0.0625
Outputs:
- scores: float32 [1024, 4], replicated
The draws below stay inside these ranges and needn't reach their ends.
All inputs are finite; a program needn't handle non-finite values.
Results may differ from the reference program's by a relative error of at most 0.008.
Values may be sent and summed in bfloat16 or wider, within the bound.
A program may use at most 128 MiB of HBM per device.

```python
import math
import jax
import jax.numpy as jnp
from jax import lax

FF = 14336
D = 8192
RANK = 32
QUERIES = 4
TOKENS = 1024


def level_of(rng, extent, split, smallest, high):
    def one(axis_at, parts):
        steps = jax.random.uniform(jax.random.fold_in(jax.random.fold_in(rng, 6), axis_at), (parts,), jnp.float32, smallest / len(split), high / len(split))
        return jnp.repeat(jnp.exp(steps), extent[axis_at] // parts).reshape((-1,) + (1,) * (len(extent) - axis_at - 1))

    level = one(*split[0])
    for cut in split[1:]:
        level = level * one(*cut)
    return level


def gaussian(rng, extent, deviation, most, cuts=(), kind=jnp.bfloat16):
    array = deviation * jax.random.normal(rng, extent, jnp.float32)
    if cuts:
        array = array * level_of(rng, extent, cuts, -0.22, 0.18)
    return jnp.clip(array, -most, most).astype(kind)


def setup_inputs(seed: int = 0) -> dict:
    keys = jax.random.split(jax.random.key(seed), 8)
    return {
        "out_grads": gaussian(keys[0], (TOKENS, FF), 1.0, 6.0, ((0, 128),)),
        "activations": gaussian(keys[1], (TOKENS, D), 1.0, 6.0, ((0, 128),)),
        "grad_basis": gaussian(keys[2], (FF, FF), FF ** -0.5, 0.046875, ((1, 32),)),
        "act_basis": gaussian(keys[3], (D, D), D ** -0.5, 0.0625, ((1, 32),)),
        "corrections": jnp.clip(jnp.exp(math.log(5.0) - 4.609084 * jax.random.uniform(keys[4], (FF, D), jnp.float32) ** level_of(keys[4], (FF, D), ((0, 32),), -0.2, 0.2)), 0.049804688, 5.0).astype(jnp.bfloat16),
        "query_left": gaussian(keys[5], (QUERIES, RANK, FF), (RANK * FF) ** -0.5, 0.0078125, ((2, 32),)),
        "query_right": gaussian(keys[6], (QUERIES, RANK, D), D ** -0.5, 0.0625, ((2, 32),)),
    }


def reference(out_grads, activations, grad_basis, act_basis, corrections, query_left, query_right):
    grad_rot = jnp.dot(out_grads, grad_basis, preferred_element_type=jnp.float32)
    act_rot = jnp.dot(activations, act_basis, preferred_element_type=jnp.float32).astype(jnp.bfloat16)
    inverse = 1.0 / (corrections.astype(jnp.float32) + 0.1)
    act_wide = act_rot.astype(jnp.float32)

    def one_query(factors):
        left, right = factors
        product = jnp.dot(left.astype(jnp.float32).T, right.astype(jnp.float32))
        precond = (product * inverse).astype(jnp.bfloat16).astype(jnp.float32)
        applied = jnp.dot(act_wide, precond.T)
        return jnp.sum(applied * grad_rot, axis=1)

    columns = lax.map(one_query, (query_left, query_right))
    return columns.T
```

```python
import jax
import jax.numpy as jnp
from jax import lax
from jax.experimental import pallas as pl
from jax.experimental.pallas import tpu as pltpu
from jax.sharding import PartitionSpec as P

MESH = pl.DeviceIdType.MESH
F32, BF16 = jnp.float32, jnp.bfloat16

FF, D, Q, R, T = 14336, 8192, 4, 32, 1024
EIG, GRP = 32, 4
ROWS = T // (EIG * GRP)
TG = T // GRP
FL, DL = FF // EIG, D // EIG
KP = D // 8
KA = D // 2
KG = FF // 2
NG = 4
KC = KG // NG
QI = Q * FL
NSEM = 112

NT = (((1,), (1,)), ((), ()))


def body(
    a_hbm, g_hbm, bt_hbm, ab_hbm, corr_hbm, ql_hbm, qr_hbm, out_ref,
    a_in, g_in, abuf, gbuf, rbuf, arbuf, pbuf, bt_v, corr_v, ql_v, lbd, inv_v,
    act_v, gr_v, acc_v, red1, red2, ssem, rsem, lsem,
):
    e = lax.axis_index("eig")
    z = lax.axis_index("grp")
    c, x, y = lax.rem(e, 2), lax.rem(e // 2, 4), e // 8
    s1, s2 = 2 + 6 * c, 8 - 6 * c
    p1, p2 = x + c * (y - x), y + c * (x - y)
    mod4 = lambda v: lax.rem(v + 4, 4)
    d1 = lambda k: {"eig": c + mod4(p1 + k) * s1 + p2 * s2}
    d2 = lambda k: {"eig": c + p1 * s1 + mod4(p2 + k) * s2}
    dz = lambda k: {"grp": mod4(z + k)}
    sib = {"eig": e + 1 - 2 * c}

    tags, sent = {}, []

    def send(tag, src, dst, dev):
        i = tags.setdefault(tag, len(tags))
        cp = pltpu.make_async_remote_copy(
            src_ref=src, dst_ref=dst, send_sem=ssem.at[i], recv_sem=rsem.at[i],
            device_id=dev, device_id_type=MESH)
        cp.start()
        sent.append(cp)

    def recv(tag, ref):
        pltpu.make_async_copy(ref, ref, rsem.at[tags[tag]]).wait()

    def local(i, src, dst):
        return pltpu.make_async_copy(src, dst, lsem.at[i])

    ld_a = local(0, a_hbm.at[:, pl.ds(pl.multiple_of(c * KA, KA), KA)], a_in.at[c])
    ld_g = local(1, g_hbm.at[:, pl.ds(pl.multiple_of(c * KG, KG), KG)], g_in.at[c])
    ld_r = local(2, qr_hbm.at[z], rbuf.at[c, z, p2, p1])
    ld_ql = local(3, ql_hbm, ql_v)

    ld_ab = [local(15 + i, ab_hbm.at[pl.ds(i * KP, KP)], pbuf.at[6 + i // 4, i % 4, pl.ds(0, KP)])
             for i in range(8)]

    def ld_bt(k, cc):
        at = cc * KG + k * KC
        return local(5 + cc, bt_hbm.at[:, pl.ds(at, KC)], bt_v.at[cc])

    def ld_corr(n, b):
        cc, row = n // 4, lax.rem(n, 4)
        eig = cc + b * (2 + 6 * cc) + row * (8 - 6 * cc)
        slot = lax.rem(n, 2)
        return local(7 + slot * 4 + b, corr_hbm.at[:, pl.ds(pl.multiple_of(eig * DL, DL), DL)],
                     corr_v.at[slot, b])

    for cp in (ld_a, ld_g, ld_r, ld_ql, *ld_ab):
        cp.start()
    for cc in range(2):
        ld_bt(0, cc).start()
    for b in range(4):
        ld_corr(0, b).start()

    barrier = pltpu.get_barrier_semaphore()
    for dev in [d1(1), d1(2), d1(3), d2(1), d2(2), d2(3), dz(1), dz(2), dz(3), sib]:
        pl.semaphore_signal(barrier, inc=1, device_id=dev, device_id_type=MESH)
    pl.semaphore_wait(barrier, 10)

    def p1_start(nm, whole):
        send(nm + "1+", whole(p1), whole(p1), d1(1))
        send(nm + "1-", whole(p1), whole(p1), d1(3))

    def p1_forward(nm, whole, half):
        left, right = mod4(p1 + 3), mod4(p1 + 1)
        recv(nm + "1+", whole(left))
        send(nm + "1f+", half(left, 0), half(left, 0), d1(1))
        recv(nm + "1-", whole(right))
        send(nm + "1f-", half(right, 1), half(right, 1), d1(3))

    def p1_end(nm, half):
        far = mod4(p1 + 2)
        recv(nm + "1f+", half(far, 0))
        recv(nm + "1f-", half(far, 1))

    def p2_start(nm, half):
        for tag, h, k in (("a+", 0, 1), ("a-", 1, 3), ("b+", 1, 1), ("b-", 0, 3)):
            send(nm + tag, half(p2, h), half(p2, h), d2(k))

    def p2_forward(nm, half):
        left, right = mod4(p2 + 3), mod4(p2 + 1)
        recv(nm + "a+", half(left, 0))
        send(nm + "2f+", half(left, 0), half(left, 0), d2(1))
        recv(nm + "a-", half(right, 1))
        send(nm + "2f-", half(right, 1), half(right, 1), d2(3))

    def p2_middle(nm, half):
        recv(nm + "b+", half(mod4(p2 + 3), 1))
        recv(nm + "b-", half(mod4(p2 + 1), 0))

    def p2_end(nm, half):
        far = mod4(p2 + 2)
        recv(nm + "2f+", half(far, 0))
        recv(nm + "2f-", half(far, 1))

    def share(nm, ref):
        send(nm, ref, ref, sib)

    a1 = lambda at: abuf.at[c, p2, at]
    a1h = lambda at, h: abuf.at[c, p2, at, :, pl.ds(h * (KA // 2), KA // 2)]
    a2h = lambda row, h: abuf.at[c, row, pl.ds(2 * h, 2)]
    g1 = lambda at: gbuf.at[c, :, p2, at]
    g1h = lambda at, h: gbuf.at[c, pl.ds(h * (NG // 2), NG // 2), p2, at]
    g2h = lambda k: lambda row, h: gbuf.at[c, k, row, pl.ds(2 * h, 2)]
    ar1 = lambda at: arbuf.at[c, p2, at]
    ar1h = lambda at, h: arbuf.at[c, p2, at, pl.ds(h * (TG // 2), TG // 2)]
    ar2h = lambda row, h: arbuf.at[c, row, pl.ds(2 * h, 2)]

    other = 1 - c
    send("sa", a_hbm.at[:, pl.ds(pl.multiple_of(other * KA, KA), KA)], a_in.at[c], sib)
    for k in (1, 3, 2):
        send(f"r1{k}", qr_hbm.at[z], rbuf.at[c, z, p2, p1], d1(k))
    send("sg", g_hbm.at[:, pl.ds(pl.multiple_of(other * KG, KG), KG)], g_in.at[c], sib)

    ld_a.wait()
    recv("sa", a_in.at[other])
    abuf[c, p2, p1] = jnp.concatenate([a_in[0].astype(F32), a_in[1].astype(F32)], axis=0).astype(BF16)
    p1_start("a", a1)
    ld_g.wait()
    recv("sg", g_in.at[other])
    for k in range(NG):
        cols = slice(k * KC, (k + 1) * KC)
        gbuf[c, k, p2, p1] = jnp.concatenate(
            [g_in[0, :, cols].astype(F32), g_in[1, :, cols].astype(F32)], axis=0).astype(BF16)
    p1_start("g", g1)

    ld_r.wait()
    for k in (1, 3, 2):
        recv(f"r1{k}", rbuf.at[c, z, p2, mod4(p1 - k)])
    for k in (1, 3, 2):
        send(f"r2{k}", rbuf.at[c, z, p2], rbuf.at[c, z, p2], d2(k))
    p1_forward("a", a1, a1h)

    ld_ql.wait()
    lt = ql_v[...].reshape(Q * R, FL).astype(F32)
    lt = jnp.concatenate([lt, jnp.zeros((Q * R, 512 - FL), F32)], axis=1).T[:FL]
    lane = lax.broadcasted_iota(jnp.int32, (FL, Q * R), 1)
    for q in range(Q):
        keep = (lane >= q * R) & (lane < (q + 1) * R)
        lbd[q * FL:(q + 1) * FL] = jnp.where(keep, lt, 0.0).astype(BF16)

    for k in (1, 3, 2):
        recv(f"r2{k}", rbuf.at[c, z, mod4(p2 - k)])
    for k in (1, 3, 2):
        send(f"rz{k}", rbuf.at[c, z], rbuf.at[c, z], dz(k))
    share("rs0", rbuf.at[c, z])

    p1_end("a", a1h)
    p2_start("a", a2h)
    share("as0", abuf.at[c, p2])
    p1_forward("g", g1, g1h)
    p1_end("g", g1h)
    p2_forward("a", a2h)
    p2_start("g0", g2h(0))
    p2_middle("a", a2h)
    share("as1", abuf.at[c, mod4(p2 + 1)])
    share("as3", abuf.at[c, mod4(p2 + 3)])
    p2_end("a", a2h)
    share("as2", abuf.at[c, mod4(p2 + 2)])
    p2_forward("g0", g2h(0))
    p2_start("g1", g2h(1))
    for k in (1, 3, 2):
        recv(f"rz{k}", rbuf.at[c, mod4(z - k)])
        share(f"rs{k}", rbuf.at[c, mod4(z - k)])

    for cp in ld_ab:
        cp.wait()
    for k in range(4):
        recv(f"as{k}", abuf.at[other, mod4(p1 + k)])
    for cc in range(2):
        for piece in range(4):
            cols = slice(piece * KP, (piece + 1) * KP)
            av = abuf[cc, :, :, :, cols]
            if cc == 1:
                av = jnp.swapaxes(av, 0, 1)
            part = jnp.dot(av.reshape(TG, KP), pbuf[6 + cc, piece, :KP], preferred_element_type=F32)
            if cc == 0 and piece == 0:
                act_v[...] = part
            else:
                act_v[...] += part
    arbuf[c, p2, p1] = act_v[...].astype(BF16)
    p1_start("r", ar1)

    for k in range(4):
        recv(f"rs{k}", rbuf.at[other, mod4(z - k)])

    def precond(n):
        cc, row = n // 4, lax.rem(n, 4)
        slot = lax.rem(n, 2)

        @pl.when(n < 7)
        def _():
            for b in range(4):
                ld_corr(n + 1, b).start()

        for b in range(4):
            ld_corr(n, b).wait()

        def one(b, _):
            inv_v[...] = 1.0 / (corr_v[slot, b].astype(F32) + 0.1)
            right = rbuf[cc, :, row, b].reshape(Q * R, DL)
            for q in range(Q):
                prod = jnp.dot(lbd[q * FL:(q + 1) * FL], right, preferred_element_type=F32)
                pbuf[n, b, q * FL:(q + 1) * FL] = (prod * inv_v[...]).astype(BF16)
            return 0

        lax.fori_loop(0, 4, one, 0)

    def preconds(lo, hi):
        lax.fori_loop(lo, hi, lambda n, _: (precond(n), 0)[1], 0)

    def grad_chunk(k):
        recv(f"gs{k}", gbuf.at[other, k])
        for cc in range(2):
            ld_bt(k, cc).wait()
            gv = gbuf[cc, k]
            if cc == 1:
                gv = jnp.swapaxes(gv, 0, 1)
            part = lax.dot_general(bt_v[cc], gv.reshape(TG, KC), NT, preferred_element_type=F32)
            if k == 0 and cc == 0:
                gr_v[...] = part
            else:
                gr_v[...] += part
            if k + 1 < NG:
                ld_bt(k + 1, cc).start()

    preconds(0, 1)
    p2_middle("g0", g2h(0))
    p2_end("g0", g2h(0))
    share("gs0", gbuf.at[c, 0])
    p2_forward("g1", g2h(1))
    p2_start("g2", g2h(2))
    p1_forward("r", ar1, ar1h)
    preconds(1, 2)
    p1_end("r", ar1h)
    share("rr0", arbuf.at[c, p2])
    p2_middle("g1", g2h(1))
    p2_end("g1", g2h(1))
    share("gs1", gbuf.at[c, 1])
    p2_forward("g2", g2h(2))
    p2_start("g3", g2h(3))
    grad_chunk(0)
    preconds(2, 4)
    p2_middle("g2", g2h(2))
    p2_end("g2", g2h(2))
    share("gs2", gbuf.at[c, 2])
    p2_forward("g3", g2h(3))
    p2_start("r", ar2h)
    grad_chunk(1)
    preconds(4, 5)
    p2_middle("g3", g2h(3))
    p2_end("g3", g2h(3))
    share("gs3", gbuf.at[c, 3])
    p2_forward("r", ar2h)
    grad_chunk(2)
    preconds(5, 8)
    grad_chunk(3)

    def applied(cc, row, first=False):
        n = cc * 4 + row
        rhs = jnp.concatenate([arbuf[cc, row, b] for b in range(4)], axis=1)

        def tile(m, _):
            rows = pl.ds(pl.multiple_of(m * FL, FL), FL)
            lhs = jnp.concatenate([pbuf[n, b, rows] for b in range(4)], axis=1)
            part = lax.dot_general(lhs, rhs, NT, preferred_element_type=F32)
            if first:
                acc_v[rows] = part
            else:
                acc_v[rows] += part
            return 0

        lax.fori_loop(0, Q, tile, 0)

    applied(c, p2, True)
    recv("rr0", arbuf.at[other, p1])
    p2_middle("r", ar2h)
    share("rr1", arbuf.at[c, mod4(p2 + 1)])
    share("rr3", arbuf.at[c, mod4(p2 + 3)])
    applied(other, p1)
    applied(c, mod4(p2 + 1))
    applied(c, mod4(p2 + 3))
    p2_end("r", ar2h)
    share("rr2", arbuf.at[c, mod4(p2 + 2)])
    for k in (1, 3):
        recv(f"rr{k}", arbuf.at[other, mod4(p1 + k)])
        applied(other, mod4(p1 + k))
    applied(c, mod4(p2 + 2))
    recv("rr2", arbuf.at[other, mod4(p1 + 2)])
    applied(other, mod4(p1 + 2))

    gr = gr_v[...]
    sc = [jnp.sum(acc_v[q * FL:(q + 1) * FL] * gr, axis=0, keepdims=True) for q in range(Q)]
    sc = jnp.concatenate(sc, axis=0)
    place1 = x * 2 + c
    red1[place1] = jnp.concatenate([sc[:, :128], sc[:, 128:]], axis=0)
    for k in range(1, 8):
        to = lax.rem(place1 + k, 8)
        send(f"s1{k}", red1.at[place1], red1.at[place1], {"eig": y * 8 + to})
    for k in range(1, 8):
        recv(f"s1{k}", red1.at[lax.rem(place1 + 8 - k, 8)])
    red2[z, y] = jnp.sum(red1[...], axis=0)
    for kz in range(4):
        for ky in range(4):
            if kz or ky:
                send(f"s2{kz}{ky}", red2.at[z, y], red2.at[z, y],
                     {"grp": mod4(z + kz), "eig": mod4(y + ky) * 8 + place1})
    for kz in range(4):
        for ky in range(4):
            if kz or ky:
                recv(f"s2{kz}{ky}", red2.at[mod4(z - kz), mod4(y - ky)])
    for g in range(GRP):
        total = jnp.sum(red2[g], axis=0)
        for half in range(2):
            out_ref[:, g * TG + half * 128:g * TG + (half + 1) * 128] = total[half * 4:half * 4 + 4]
    for cp in sent:
        cp.wait_send()
    assert len(tags) <= NSEM, len(tags)


def per_device(out_grads, activations, grad_basis, act_basis, corrections, query_left, query_right):
    any_, vmem = pl.BlockSpec(memory_space=pl.ANY), pl.BlockSpec(memory_space=pltpu.VMEM)
    out = pl.pallas_call(
        body,
        out_shape=jax.ShapeDtypeStruct((Q, T), F32),
        in_specs=[any_] * 7,
        out_specs=vmem,
        scratch_shapes=[
            pltpu.VMEM((2, ROWS, KA), BF16),
            pltpu.VMEM((2, ROWS, KG), BF16),
            pltpu.VMEM((2, 4, 4, 16, KA), BF16),
            pltpu.VMEM((2, NG, 4, 4, 16, KC), BF16),
            pltpu.VMEM((2, Q, 4, 4, R, DL), BF16),
            pltpu.VMEM((2, 4, 4, TG, DL), BF16),
            pltpu.VMEM((8, 4, QI, DL), BF16),
            pltpu.VMEM((2, FL, KC), BF16),
            pltpu.VMEM((2, 4, FL, DL), BF16),
            pltpu.VMEM((Q, R, FL), BF16),
            pltpu.VMEM((QI, Q * R), BF16),
            pltpu.VMEM((FL, DL), F32),
            pltpu.VMEM((TG, DL), F32),
            pltpu.VMEM((FL, TG), F32),
            pltpu.VMEM((QI, TG), F32),
            pltpu.VMEM((8, 8, 128), F32),
            pltpu.VMEM((GRP, 4, 8, 128), F32),
            pltpu.SemaphoreType.DMA((NSEM,)),
            pltpu.SemaphoreType.DMA((NSEM,)),
            pltpu.SemaphoreType.DMA((23,)),
        ],
        compiler_params=pltpu.CompilerParams(
            collective_id=0, has_side_effects=True, vmem_limit_bytes=60 * 1024 * 1024),
    )(activations, out_grads, grad_basis.T, act_basis, corrections, query_left, query_right)
    return out.T


def solution(mesh):
    placed = (
        P(("grp", "eig"), None),
        P(("grp", "eig"), None),
        P(None, "eig"),
        P(None, "eig"),
        P("eig", None),
        P(None, None, "eig"),
        P(None, None, "eig"),
    )
    return jax.shard_map(per_device, mesh=mesh, in_specs=placed, out_specs=P(), check_vma=False)
```

```python
import jax
import jax.numpy as jnp
from jax import lax
from jax.experimental import pallas as pl
from jax.experimental.pallas import tpu as pltpu
from jax.sharding import PartitionSpec as P

MESH = pl.DeviceIdType.MESH
F32, BF16 = jnp.float32, jnp.bfloat16

FF, D, Q, R, T = 14336, 8192, 4, 32, 1024
EIG, GRP = 32, 4
ROWS = T // (EIG * GRP)
TG = T // GRP
FL, DL = FF // EIG, D // EIG
KP = D // 8
KA = D // 2
KG = FF // 2
NG = 2
KC = KG // NG
KB = KC // 2
QI = Q * FL
QP = 2 * FL
NSEM = 120

NT = (((1,), (1,)), ((), ()))


def body(
    a_hbm, g_hbm, bt_hbm, ab_hbm, corr_hbm, ql_hbm, qr_hbm, out_ref,
    a_in, g_in, abuf, gbuf, rbuf, arbuf, pbuf, bt_v, ab_v, ql_v, lbd, inv_v,
    act_v, gr_v, acc_v, red1, red2, ssem, rsem, lsem,
):
    e = lax.axis_index("eig")
    z = lax.axis_index("grp")
    c, x, y = lax.rem(e, 2), lax.rem(e // 2, 4), e // 8
    s1, s2 = 2 + 6 * c, 8 - 6 * c
    p1, p2 = x + c * (y - x), y + c * (x - y)
    mod4 = lambda v: lax.rem(v + 4, 4)
    d1 = lambda k: {"eig": c + mod4(p1 + k) * s1 + p2 * s2}
    d2 = lambda k: {"eig": c + p1 * s1 + mod4(p2 + k) * s2}
    dz = lambda k: {"grp": mod4(z + k)}
    sib = {"eig": e + 1 - 2 * c}

    tags, sent = {}, []

    def send(tag, src, dst, dev):
        i = tags.setdefault(tag, len(tags))
        cp = pltpu.make_async_remote_copy(
            src_ref=src, dst_ref=dst, send_sem=ssem.at[i], recv_sem=rsem.at[i],
            device_id=dev, device_id_type=MESH)
        cp.start()
        sent.append(cp)

    def recv(tag, ref):
        pltpu.make_async_copy(ref, ref, rsem.at[tags[tag]]).wait()

    def local(i, src, dst):
        return pltpu.make_async_copy(src, dst, lsem.at[i])

    ld_a = local(0, a_hbm.at[:, pl.ds(pl.multiple_of(c * KA, KA), KA)], a_in.at[c])
    ld_g = local(1, g_hbm.at[:, pl.ds(pl.multiple_of(c * KG, KG), KG)], g_in.at[c])
    pair = lax.rem(z, 2)
    r_own = qr_hbm.at[pl.ds(2 * pair, 2)]
    ld_r = local(2, r_own, rbuf.at[c, pair, p2, p1])
    ld_ql = local(3, ql_hbm, ql_v)

    def ld_ab(i):
        return local(7 + i % 4, ab_hbm.at[pl.ds(i * KP, KP)], ab_v.at[i % 4])

    def ld_bt(i):
        k, cc, h = i // 4, i // 2 % 2, i % 2
        return local(5 + i % 2, bt_hbm.at[:, pl.ds(cc * KG + k * KC + h * KB, KB)], bt_v.at[i % 2])

    def ld_corr(n, b):
        cc, row = n // 4, lax.rem(n, 4)
        eig = cc + b * (2 + 6 * cc) + row * (8 - 6 * cc)
        return local(11 + n * 4 + b, corr_hbm.at[:, pl.ds(pl.multiple_of(eig * DL, DL), DL)],
                     pbuf.at[n, b, pl.ds(pl.multiple_of((1 - pair) * QP, QP), FL)])

    for cp in (ld_a, ld_g, ld_r, ld_ql):
        cp.start()
    for i in range(4):
        ld_ab(i).start()
    for i in range(2):
        ld_bt(i).start()

    def start_corr(n, _):
        for b in range(4):
            ld_corr(n, b).start()
        return 0

    lax.fori_loop(0, 8, start_corr, 0)

    barrier = pltpu.get_barrier_semaphore()
    for dev in [d1(1), d1(2), d1(3), d2(1), d2(2), d2(3), dz(1), dz(2), dz(3), sib]:
        pl.semaphore_signal(barrier, inc=1, device_id=dev, device_id_type=MESH)
    pl.semaphore_wait(barrier, 10)

    left1, right1, far1 = mod4(p1 + 3), mod4(p1 + 1), mod4(p1 + 2)
    left2, right2, far2 = mod4(p2 + 3), mod4(p2 + 1), mod4(p2 + 2)
    place = {"o": p1, "l": left1, "r": right1, "f": far1}

    class Gather:
        def __init__(self, nm, blk, half):
            self.nm, self.blk, self.half = nm, blk, half

        def _send(self, tag, ref, dev):
            send(self.nm + tag, ref, ref, dev)

        def first(self):
            own = self.blk(p2, p1)
            self._send("1+", own, d1(1))
            self._send("1-", own, d1(3))

        def first_forward(self, b):
            if b == "l":
                recv(self.nm + "1+", self.blk(p2, left1))
                self._send("1f+", self.half(left1, 0), d1(1))
            else:
                recv(self.nm + "1-", self.blk(p2, right1))
                self._send("1f-", self.half(right1, 1), d1(3))

        def first_far(self):
            recv(self.nm + "1f+", self.half(far1, 0))
            recv(self.nm + "1f-", self.half(far1, 1))

        def second(self, b):
            ref = self.blk(p2, place[b])
            self._send("2+" + b, ref, d2(1))
            self._send("2-" + b, ref, d2(3))

        def forward(self, b):
            if b in "of":
                recv(self.nm + "2+" + b, self.blk(left2, place[b]))
                self._send("2f" + b, self.blk(left2, place[b]), d2(1))
            else:
                recv(self.nm + "2-" + b, self.blk(right2, place[b]))
                self._send("2f" + b, self.blk(right2, place[b]), d2(3))

        def share(self, k):
            self._send(f"s{k}", self.row(c, mod4(p2 + k)), sib)

        def near_row(self, b):
            if b == "l":
                recv(self.nm + "2+l", self.blk(left2, left1))
                recv(self.nm + "2+r", self.blk(left2, right1))
                self.share(3)
            else:
                recv(self.nm + "2-o", self.blk(right2, p1))
                recv(self.nm + "2-f", self.blk(right2, far1))
                self.share(1)

        def far_row(self):
            for b in "olrf":
                recv(self.nm + "2f" + b, self.blk(far2, place[b]))
            self.share(2)

        def shared(self, k):
            recv(f"{self.nm}s{k}", self.row(other, mod4(p1 + k)))

        def all_shared(self):
            for k in range(4):
                self.shared(k)

    other = 1 - c
    ga = Gather("a", lambda row, at: abuf.at[c, row, at],
                lambda at, h: abuf.at[c, p2, at, :, pl.ds(h * (KA // 2), KA // 2)])
    ga.row = lambda cc, row: abuf.at[cc, row]

    def gather_g(k):
        g = Gather(f"g{k}", lambda row, at: gbuf.at[c, k, row, at],
                   lambda at, h: gbuf.at[c, k, p2, at, :, pl.ds(h * (KC // 2), KC // 2)])
        g.row = lambda cc, row: gbuf.at[cc, k, row]
        return g

    g0, g1 = gather_g(0), gather_g(1)
    gt = Gather("t", lambda row, at: arbuf.at[c, row, at],
                 lambda at, h: arbuf.at[c, p2, at, pl.ds(h * (TG // 2), TG // 2)])
    gt.row = lambda cc, row: arbuf.at[cc, row]

    def act_rot():
        ga.all_shared()
        for i in range(8):
            cc = i // 4
            ld_ab(i).wait()
            av = abuf[cc, :, :, :, i % 4 * KP:(i % 4 + 1) * KP]
            if cc == 1:
                av = jnp.swapaxes(av, 0, 1)
            part = jnp.dot(av.reshape(TG, KP), ab_v[i % 4], preferred_element_type=F32)
            if i == 0:
                act_v[...] = part
            else:
                act_v[...] += part
            if i < 4:
                ld_ab(i + 4).start()
        arbuf[c, p2, p1] = act_v[...].astype(BF16)

    def precond(second, n):
        at = 1 - pair if second else pair
        cc, row = n // 4, lax.rem(n, 4)
        if not second:
            for b in range(4):
                ld_corr(n, b).wait()

        def one(b, _):
            corr = pbuf[n, b, pl.ds(pl.multiple_of((1 - pair) * QP, QP), FL)]
            inv_v[...] = 1.0 / (corr.astype(F32) + 0.1)
            right = rbuf[cc, at, row, b].reshape(2 * R, DL)
            for q in range(2):
                prod = jnp.dot(lbd[at, q * FL:(q + 1) * FL], right, preferred_element_type=F32)
                pbuf[n, b, pl.ds(pl.multiple_of(at * QP + q * FL, FL), FL)] = (prod * inv_v[...]).astype(BF16)
            return 0

        lax.fori_loop(0, 4, one, 0)

    def preconds(second, lo, hi):
        lax.fori_loop(lo, hi, lambda n, _: (precond(second, n), 0)[1], 0)

    def grad_piece(i):
        k, cc, h = i // 4, i // 2 % 2, i % 2
        ld_bt(i).wait()
        gv = gbuf[cc, k, :, :, :, h * KB:(h + 1) * KB]
        if cc == 1:
            gv = jnp.swapaxes(gv, 0, 1)
        part = lax.dot_general(bt_v[i % 2], gv.reshape(TG, KB), NT, preferred_element_type=F32)
        if i == 0:
            gr_v[...] = part
        else:
            gr_v[...] += part
        if i + 2 < 8:
            ld_bt(i + 2).start()

    def applied(groups):
        def group(i, _):
            cc, row = groups[0]
            for at, (cc_at, row_at) in enumerate(groups):
                cc, row = jnp.where(i == at, cc_at, cc), jnp.where(i == at, row_at, row)
            rhs = jnp.concatenate([arbuf[cc, row, b] for b in range(4)], axis=1)
            for m in range(7):
                rows = slice(m * 256, (m + 1) * 256)
                lhs = jnp.concatenate([pbuf[cc * 4 + row, b, rows] for b in range(4)], axis=1)
                acc_v[rows] += lax.dot_general(lhs, rhs, NT, preferred_element_type=F32)
            return 0

        lax.fori_loop(0, len(groups), group, 0)

    def share_pair(k):
        ref = rbuf.at[c, 1 - pair, :, :, k // 2]
        recv(f"rz{k}", ref)
        send(f"rs{k}", ref, ref, sib)

    def left_factors():
        ld_ql.wait()
        for at in range(2):
            lt = ql_v[2 * at:2 * at + 2].reshape(2 * R, FL).astype(F32)
            lt = jnp.concatenate([lt, jnp.zeros((2 * R, 512 - FL), F32)], axis=1)
            lt = jnp.concatenate([lt, jnp.zeros((2 * R, 512), F32)], axis=0).T[:FL]
            lane = lax.broadcasted_iota(jnp.int32, (FL, 4 * R), 1)
            for q in range(2):
                keep = (lane >= q * R) & (lane < (q + 1) * R)
                lbd[at, q * FL:(q + 1) * FL] = jnp.where(keep, lt, 0.0)[:, :2 * R].astype(BF16)

        acc_v[...] = jnp.zeros_like(acc_v)

    def own_activations():
        ld_a.wait()
        recv("sa", a_in.at[other])
        abuf[c, p2, p1] = jnp.concatenate([a_in[0].astype(F32), a_in[1].astype(F32)], axis=0).astype(BF16)

    def own_out_grads():
        ld_g.wait()
        recv("sg", g_in.at[other])
        for k in range(NG):
            cols = slice(k * KC, (k + 1) * KC)
            gbuf[c, k, p2, p1] = jnp.concatenate(
                [g_in[0, :, cols].astype(F32), g_in[1, :, cols].astype(F32)], axis=0).astype(BF16)

    def right_rows():
        ld_r.wait()
        for k in (1, 3, 2):
            recv(f"r1{k}", rbuf.at[c, pair, p2, mod4(p1 - k)])
        for k in (1, 3, 2):
            send(f"r2{k}", rbuf.at[c, pair, p2], rbuf.at[c, pair, p2], d2(k))

    def right_along_z():
        for k in (1, 3, 2):
            recv(f"r2{k}", rbuf.at[c, pair, mod4(p2 - k)])
        for k in (1, 3):
            ref = rbuf.at[c, pair, :, :, k // 2]
            send(f"rz{k}", ref, ref, dz(k))
        send("rs0", rbuf.at[c, pair], rbuf.at[c, pair], sib)

    send("sa", a_hbm.at[:, pl.ds(pl.multiple_of(other * KA, KA), KA)], a_in.at[c], sib)
    for k in (1, 3, 2):
        send(f"r1{k}", r_own, rbuf.at[c, pair, p2, p1], d1(k))
    send("sg", g_hbm.at[:, pl.ds(pl.multiple_of(other * KG, KG), KG)], g_in.at[c], sib)
    left_factors()
    own_activations()
    ga.first()
    own_out_grads()
    g0.first()
    right_rows()
    ga.second("o")
    ga.first_forward("r")
    ga.first_forward("l")
    ga.second("l")
    g0.first_forward("r")
    ga.first_far()
    ga.second("f")
    ga.share(0)
    g0.first_forward("l")
    ga.second("r")
    right_along_z()
    recv("rs0", rbuf.at[other, pair])
    preconds(False, 0, 2)
    ga.forward("o")
    ga.forward("l")
    g1.first()
    ga.forward("r")
    ga.forward("f")
    ga.near_row("l")
    g0.second("l")
    g0.first_far()
    g0.second("f")
    g0.second("r")
    preconds(False, 2, 4)
    share_pair(1)
    g0.second("o")
    share_pair(3)
    g1.first_forward("l")
    g1.second("l")
    g1.first_forward("r")
    g1.second("o")
    g1.second("r")
    ga.near_row("r")
    ga.far_row()
    for k in (1, 3):
        recv(f"rs{k}", rbuf.at[other, 1 - pair, :, :, k // 2])
    preconds(False, 4, 6)
    g0.forward("l")
    act_rot()
    gt.second("o")
    g0.forward("r")
    gt.first()
    preconds(True, 0, 4)
    g0.forward("f")
    preconds(False, 6, 8)
    g0.forward("o")
    g0.near_row("r")
    g0.share(0)
    gt.first_forward("r")
    gt.first_forward("l")
    g0.near_row("l")
    g1.first_far()
    g1.share(0)
    g1.second("f")
    preconds(True, 4, 6)
    gt.second("l")
    preconds(True, 6, 8)
    gt.first_far()
    gt.second("f")
    gt.second("r")
    g1.forward("l")
    g1.forward("o")
    g0.far_row()
    gt.share(0)
    applied([(c, p2)])
    g1.forward("r")
    g1.near_row("r")
    g0.all_shared()
    grad_piece(0)
    grad_piece(1)
    gt.shared(0)
    g1.forward("f")
    g1.near_row("l")
    gt.forward("o")
    gt.forward("l")
    applied([(other, p1)])
    grad_piece(2)
    grad_piece(3)
    gt.forward("f")
    gt.near_row("l")
    applied([(c, left2)])
    gt.forward("r")
    gt.near_row("r")
    applied([(c, right2)])
    g1.far_row()
    gt.shared(3)
    applied([(other, left1)])
    gt.shared(1)
    applied([(other, right1)])
    g1.all_shared()
    grad_piece(4)
    grad_piece(5)
    gt.far_row()
    applied([(c, far2)])
    grad_piece(6)
    grad_piece(7)
    gt.shared(2)
    applied([(other, far1)])

    gr = gr_v[...]
    sc = [jnp.sum(acc_v[q * FL:(q + 1) * FL] * gr, axis=0, keepdims=True) for q in range(Q)]
    sc = jnp.concatenate(sc, axis=0)
    place1 = x * 2 + c
    red1[place1] = jnp.concatenate([sc[:, :128], sc[:, 128:]], axis=0)
    for k in range(1, 8):
        to = lax.rem(place1 + k, 8)
        send(f"s1{k}", red1.at[place1], red1.at[place1], {"eig": y * 8 + to})
    for k in range(1, 8):
        recv(f"s1{k}", red1.at[lax.rem(place1 + 8 - k, 8)])
    red2[z, y] = jnp.sum(red1[...], axis=0)
    for kz in range(4):
        for ky in range(4):
            if kz or ky:
                send(f"s2{kz}{ky}", red2.at[z, y], red2.at[z, y],
                     {"grp": mod4(z + kz), "eig": mod4(y + ky) * 8 + place1})
    for kz in range(4):
        for ky in range(4):
            if kz or ky:
                recv(f"s2{kz}{ky}", red2.at[mod4(z - kz), mod4(y - ky)])
    for g in range(GRP):
        total = jnp.sum(red2[g], axis=0)
        for half in range(2):
            out_ref[:, g * TG + half * 128:g * TG + (half + 1) * 128] = total[half * 4:half * 4 + 4]
    for cp in sent:
        cp.wait_send()
    assert len(tags) <= NSEM, len(tags)


def per_device(out_grads, activations, grad_basis, act_basis, corrections, query_left, query_right):
    any_, vmem = pl.BlockSpec(memory_space=pl.ANY), pl.BlockSpec(memory_space=pltpu.VMEM)
    out = pl.pallas_call(
        body,
        out_shape=jax.ShapeDtypeStruct((Q, T), F32),
        in_specs=[any_] * 7,
        out_specs=vmem,
        scratch_shapes=[
            pltpu.VMEM((2, ROWS, KA), BF16),
            pltpu.VMEM((2, ROWS, KG), BF16),
            pltpu.VMEM((2, 4, 4, 16, KA), BF16),
            pltpu.VMEM((2, NG, 4, 4, 16, KC), BF16),
            pltpu.VMEM((2, 2, 4, 4, 2, R, DL), BF16),
            pltpu.VMEM((2, 4, 4, TG, DL), BF16),
            pltpu.VMEM((8, 4, QI, DL), BF16),
            pltpu.VMEM((2, FL, KB), BF16),
            pltpu.VMEM((4, KP, DL), BF16),
            pltpu.VMEM((Q, R, FL), BF16),
            pltpu.VMEM((2, QP, 2 * R), BF16),
            pltpu.VMEM((FL, DL), F32),
            pltpu.VMEM((TG, DL), F32),
            pltpu.VMEM((FL, TG), F32),
            pltpu.VMEM((QI, TG), F32),
            pltpu.VMEM((8, 8, 128), F32),
            pltpu.VMEM((GRP, 4, 8, 128), F32),
            pltpu.SemaphoreType.DMA((NSEM,)),
            pltpu.SemaphoreType.DMA((NSEM,)),
            pltpu.SemaphoreType.DMA((43,)),
        ],
        compiler_params=pltpu.CompilerParams(
            collective_id=0, has_side_effects=True, vmem_limit_bytes=60 * 1024 * 1024),
    )(activations, out_grads, grad_basis.T, act_basis, corrections, query_left, query_right)
    return out.T


def solution(mesh):
    placed = (
        P(("grp", "eig"), None),
        P(("grp", "eig"), None),
        P(None, "eig"),
        P(None, "eig"),
        P("eig", None),
        P(None, None, "eig"),
        P(None, None, "eig"),
    )
    return jax.shard_map(per_device, mesh=mesh, in_specs=placed, out_specs=P(), check_vma=False)
```

```python
import jax
import jax.numpy as jnp
from jax import lax
from jax.experimental import pallas as pl
from jax.experimental.pallas import tpu as pltpu
from jax.sharding import PartitionSpec as P

MESH = pl.DeviceIdType.MESH
F32, BF16 = jnp.float32, jnp.bfloat16

FF, D, Q, R, T = 14336, 8192, 4, 32, 1024
EIG, GRP = 32, 4
ROWS = T // (EIG * GRP)
TG = T // GRP
FL, DL = FF // EIG, D // EIG
KP = D // 8
KA = D // 2
KG = FF // 2
NG = 2
KC = KG // NG
KB = KC // 2
QI = Q * FL
QP = 2 * FL
NSEM = 120

NT = (((1,), (1,)), ((), ()))


def body(
    a_hbm, g_hbm, bt_hbm, ab_hbm, corr_hbm, ql_hbm, qr_hbm, out_ref,
    a_in, g_in, abuf, gbuf, rbuf, arbuf, pbuf, bt_v, ab_v, ql_v, lbd, inv_v,
    act_v, gr_v, acc_v, red1, red2, ssem, rsem, lsem,
):
    e = lax.axis_index("eig")
    z = lax.axis_index("grp")
    c, x, y = lax.rem(e, 2), lax.rem(e // 2, 4), e // 8
    s1, s2 = 2 + 6 * c, 8 - 6 * c
    p1, p2 = x + c * (y - x), y + c * (x - y)
    mod4 = lambda v: lax.rem(v + 4, 4)
    d1 = lambda k: {"eig": c + mod4(p1 + k) * s1 + p2 * s2}
    d2 = lambda k: {"eig": c + p1 * s1 + mod4(p2 + k) * s2}
    dz = lambda k: {"grp": mod4(z + k)}
    sib = {"eig": e + 1 - 2 * c}

    tags, sent = {}, []

    def send(tag, src, dst, dev):
        i = tags.setdefault(tag, len(tags))
        cp = pltpu.make_async_remote_copy(
            src_ref=src, dst_ref=dst, send_sem=ssem.at[i], recv_sem=rsem.at[i],
            device_id=dev, device_id_type=MESH)
        cp.start()
        sent.append(cp)

    def recv(tag, ref):
        pltpu.make_async_copy(ref, ref, rsem.at[tags[tag]]).wait()

    def local(i, src, dst):
        return pltpu.make_async_copy(src, dst, lsem.at[i])

    ld_a = local(0, a_hbm.at[:, pl.ds(pl.multiple_of(c * KA, KA), KA)], a_in.at[c])
    ld_g = local(1, g_hbm.at[:, pl.ds(pl.multiple_of(c * KG, KG), KG)], g_in.at[c])
    pair = lax.rem(z, 2)
    r_own = qr_hbm.at[pl.ds(2 * pair, 2)]
    ld_r = local(2, r_own, rbuf.at[c, pair, p2, p1])
    ld_ql = local(3, ql_hbm, ql_v)

    def ld_ab(cc, i):
        at = pl.multiple_of((cc * 4 + i) * KP, KP)
        return local(7 + i, ab_hbm.at[pl.ds(at, KP)], ab_v.at[i])

    def ld_bt(i):
        k, cc, h = i // 4, i // 2 % 2, i % 2
        return local(5 + i % 2, bt_hbm.at[:, pl.ds(cc * KG + k * KC + h * KB, KB)], bt_v.at[i % 2])

    def ld_corr(n, b):
        cc, row = n // 4, lax.rem(n, 4)
        eig = cc + b * (2 + 6 * cc) + row * (8 - 6 * cc)
        return local(11 + n * 4 + b, corr_hbm.at[:, pl.ds(pl.multiple_of(eig * DL, DL), DL)],
                     pbuf.at[n, b, pl.ds(pl.multiple_of((1 - pair) * QP, QP), FL)])

    for cp in (ld_a, ld_g, ld_r, ld_ql):
        cp.start()
    def large_loads():
        def corr(n, _):
            for b in range(4):
                ld_corr(n, b).start()
            return 0

        lax.fori_loop(0, 8, corr, 0)
        for i in range(4):
            ld_ab(c, i).start()
        for i in range(2):
            ld_bt(i).start()

    barrier = pltpu.get_barrier_semaphore()
    for dev in (d1(1), d1(2), d1(3), d2(1), d2(3), dz(1), dz(3), sib):
        pl.semaphore_signal(barrier, inc=1, device_id=dev, device_id_type=MESH)
    pl.semaphore_wait(barrier, 8)

    left1, right1, far1 = mod4(p1 + 3), mod4(p1 + 1), mod4(p1 + 2)
    left2, right2, far2 = mod4(p2 + 3), mod4(p2 + 1), mod4(p2 + 2)
    place = {"o": p1, "l": left1, "r": right1, "f": far1}
    place2 = {"o": p2, "l": left2, "r": right2, "f": far2}

    class Gather:
        def __init__(self, nm, blk, half):
            self.nm, self.blk, self.half = nm, blk, half

        def _send(self, tag, ref, dev):
            send(self.nm + tag, ref, ref, dev)

        def first(self):
            own = self.blk(p2, p1)
            self._send("1+", own, d1(1))
            self._send("1-", own, d1(3))

        def first_forward(self, b):
            if b == "l":
                recv(self.nm + "1+", self.blk(p2, left1))
                self._send("1f+", self.half(left1, 0), d1(1))
            else:
                recv(self.nm + "1-", self.blk(p2, right1))
                self._send("1f-", self.half(right1, 1), d1(3))

        def first_far(self):
            recv(self.nm + "1f+", self.half(far1, 0))
            recv(self.nm + "1f-", self.half(far1, 1))

        def second(self, b):
            ref = self.blk(p2, place[b])
            self._send("2+" + b, ref, d2(1))
            self._send("2-" + b, ref, d2(3))

        def forward(self, b):
            if b in "of":
                recv(self.nm + "2+" + b, self.blk(left2, place[b]))
                self._send("2f" + b, self.blk(left2, place[b]), d2(1))
            else:
                recv(self.nm + "2-" + b, self.blk(right2, place[b]))
                self._send("2f" + b, self.blk(right2, place[b]), d2(3))

        def share(self, k):
            self._send(f"s{k}", self.row(c, mod4(p2 + k)), sib)

        def near_row(self, b):
            if b == "l":
                recv(self.nm + "2+l", self.blk(left2, left1))
                recv(self.nm + "2+r", self.blk(left2, right1))
                self.share(3)
            else:
                recv(self.nm + "2-o", self.blk(right2, p1))
                recv(self.nm + "2-f", self.blk(right2, far1))
                self.share(1)

        def far_row(self):
            for b in "olrf":
                recv(self.nm + "2f" + b, self.blk(far2, place[b]))
            self.share(2)

        def far_block(self, b):
            ref = self.blk(far2, place[b])
            recv(self.nm + "2f" + b, ref)
            self._send("s2" + b, ref, sib)

        def shared_block(self, b):
            recv(self.nm + "s2" + b, self.blk(far1, place2[b], other))

        def shared(self, k):
            recv(f"{self.nm}s{k}", self.row(other, mod4(p1 + k)))

        def all_shared(self):
            for k in range(4):
                self.shared(k)

    other = 1 - c
    ga = Gather("a", lambda row, at: abuf.at[c, row, at],
                lambda at, h: abuf.at[c, p2, at, :, pl.ds(h * (KA // 2), KA // 2)])
    ga.row = lambda cc, row: abuf.at[cc, row]

    def gather_g(k):
        g = Gather(f"g{k}", lambda row, at: gbuf.at[c, k, row, at],
                   lambda at, h: gbuf.at[c, k, p2, at, :, pl.ds(h * (KC // 2), KC // 2)])
        g.row = lambda cc, row: gbuf.at[cc, k, row]
        return g

    g0, g1 = gather_g(0), gather_g(1)
    gt = Gather("t", lambda row, at, cc=c: arbuf.at[cc, row, at],
                 lambda at, h: arbuf.at[c, p2, at, pl.ds(h * (TG // 2), TG // 2)])
    gt.row = lambda cc, row: arbuf.at[cc, row]

    def act_half(cc, more):
        total = None
        for i in range(4):
            ld_ab(0, i).wait()
            av = abuf[cc, :, :, :, i * KP:(i + 1) * KP].reshape(TG, KP)
            part = jnp.dot(av, ab_v[i], preferred_element_type=F32)
            total = part if i == 0 else total + part
            if more:
                ld_ab(other, i).start()
        act_v[cc] = total

    def act_rot_own():
        act_half(c, True)

    def act_rot_other():
        ga.all_shared()
        act_half(other, False)
        turned = jnp.swapaxes(act_v[1].reshape(4, 4, 16, DL), 0, 1).reshape(TG, DL)
        arbuf[c, p2, p1] = (act_v[0] + turned).astype(BF16)

    def precond(second, n):
        at = 1 - pair if second else pair
        cc, row = n // 4, lax.rem(n, 4)
        if not second:
            for b in range(4):
                ld_corr(n, b).wait()

        for b in range(4):
            corr = pbuf[n, b, pl.ds(pl.multiple_of((1 - pair) * QP, QP), FL)]
            inv_v[b] = 1.0 / (corr.astype(F32) + 0.1)
        right = jnp.concatenate([rbuf[cc, at, row, b].reshape(2 * R, DL) for b in range(4)], axis=1)
        for q in range(2):
            prod = jnp.dot(lbd[at, q * FL:(q + 1) * FL], right, preferred_element_type=F32)
            for b in range(4):
                pbuf[n, b, pl.ds(pl.multiple_of(at * QP + q * FL, FL), FL)] = (
                    prod[:, b * DL:(b + 1) * DL] * inv_v[b]).astype(BF16)

    def preconds(second, lo, hi):
        for n in range(lo, hi):
            precond(second, n)

    def grad_piece(i):
        k, cc, h = i // 4, i // 2 % 2, i % 2
        ld_bt(i).wait()
        gv = gbuf[cc, k, :, :, :, h * KB:(h + 1) * KB]
        if cc == 1:
            gv = jnp.swapaxes(gv, 0, 1)
        part = lax.dot_general(bt_v[i % 2], gv.reshape(TG, KB), NT, preferred_element_type=F32)
        if i == 0:
            gr_v[...] = part
        else:
            gr_v[...] += part
        if i + 2 < 8:
            ld_bt(i + 2).start()

    def applied(groups):
        for cc, row in groups:
            applied_blocks(cc, row, range(4))

    def applied_blocks(cc, row, ats):
        rhs = jnp.concatenate([arbuf[cc, row, at] for at in ats], axis=1)
        for m in range(7):
            rows = slice(m * 256, (m + 1) * 256)
            lhs = jnp.concatenate([pbuf[cc * 4 + row, at, rows] for at in ats], axis=1)
            acc_v[rows] += lax.dot_general(lhs, rhs, NT, preferred_element_type=F32)

    def share_pair(k):
        ref = rbuf.at[c, 1 - pair, :, :, k // 2]
        recv(f"rz{k}", ref)
        send(f"rs{k}", ref, ref, sib)

    def left_factors():
        ld_ql.wait()
        for at in range(2):
            lt = ql_v[2 * at:2 * at + 2].reshape(2 * R, FL).astype(F32)
            lt = jnp.concatenate([lt, jnp.zeros((2 * R, 512 - FL), F32)], axis=1)
            lt = jnp.concatenate([lt, jnp.zeros((2 * R, 512), F32)], axis=0).T[:FL]
            lane = lax.broadcasted_iota(jnp.int32, (FL, 4 * R), 1)
            for q in range(2):
                keep = (lane >= q * R) & (lane < (q + 1) * R)
                lbd[at, q * FL:(q + 1) * FL] = jnp.where(keep, lt, 0.0)[:, :2 * R].astype(BF16)

        acc_v[...] = jnp.zeros_like(acc_v)

    def own_activations():
        ld_a.wait()
        recv("sa", a_in.at[other])
        abuf[c, p2, p1] = jnp.concatenate([a_in[0].astype(F32), a_in[1].astype(F32)], axis=0).astype(BF16)

    def own_out_grads():
        ld_g.wait()
        recv("sg", g_in.at[other])
        for k in range(NG):
            cols = slice(k * KC, (k + 1) * KC)
            gbuf[c, k, p2, p1] = jnp.concatenate(
                [g_in[0, :, cols].astype(F32), g_in[1, :, cols].astype(F32)], axis=0).astype(BF16)

    def right_rows():
        ld_r.wait()
        for k in (1, 3, 2):
            recv(f"r1{k}", rbuf.at[c, pair, p2, mod4(p1 - k)])
        for k, dev in (("+", d2(1)), ("-", d2(3))):
            send("r2" + k, rbuf.at[c, pair, p2], rbuf.at[c, pair, p2], dev)

    def right_half(row, h):
        return rbuf.at[c, pair, row, pl.ds(2 * h, 2)]

    def right_forward():
        recv("r2+", rbuf.at[c, pair, left2])
        send("r2f+", right_half(left2, 0), right_half(left2, 0), d2(1))
        recv("r2-", rbuf.at[c, pair, right2])
        send("r2f-", right_half(right2, 1), right_half(right2, 1), d2(3))

    def right_along_z():
        recv("r2f+", right_half(far2, 0))
        recv("r2f-", right_half(far2, 1))
        for k in (1, 3):
            ref = rbuf.at[c, pair, :, :, k // 2]
            send(f"rz{k}", ref, ref, dz(k))
        send("rs0", rbuf.at[c, pair], rbuf.at[c, pair], sib)

    send("sa", a_hbm.at[:, pl.ds(pl.multiple_of(other * KA, KA), KA)], a_in.at[c], sib)
    for k in (1, 3, 2):
        send(f"r1{k}", r_own, rbuf.at[c, pair, p2, p1], d1(k))
    send("sg", g_hbm.at[:, pl.ds(pl.multiple_of(other * KG, KG), KG)], g_in.at[c], sib)
    own_activations()
    ga.first()
    own_out_grads()
    g0.first()
    right_rows()
    ga.first_forward("r")
    ga.second("o")
    large_loads()
    ga.second("r")
    ga.first_forward("l")
    ga.second("l")
    ga.first_far()
    ga.second("f")
    left_factors()
    right_forward()
    g0.first_forward("l")
    g0.first_forward("r")
    ga.forward("l")
    ga.forward("o")
    g1.first()
    ga.forward("r")
    ga.near_row("r")
    ga.forward("f")
    g0.second("l")
    g0.second("r")
    ga.share(0)
    right_along_z()
    recv("rs0", rbuf.at[other, pair])
    g0.second("o")
    preconds(False, 0, 2)
    ga.near_row("l")
    ga.far_row()
    g0.first_far()
    g0.second("f")
    preconds(False, 2, 4)
    g1.first_forward("l")
    g1.second("l")
    g1.first_forward("r")
    g1.second("r")
    act_rot_own()
    act_rot_other()
    gt.first()
    preconds(False, 4, 6)
    share_pair(3)
    g0.forward("f")
    share_pair(1)
    g1.second("o")
    g0.forward("r")
    preconds(False, 6, 8)
    g0.forward("o")
    g1.first_far()
    g0.forward("l")
    g1.share(0)
    g0.near_row("r")
    gt.second("o")
    gt.first_forward("r")
    gt.first_forward("l")
    for k in (1, 3):
        recv(f"rs{k}", rbuf.at[other, 1 - pair, :, :, k // 2])
    preconds(True, 0, 2)
    g0.share(0)
    gt.second("l")
    preconds(True, 2, 4)
    g0.near_row("l")
    preconds(True, 4, 6)
    gt.second("r")
    g1.second("f")
    gt.first_far()
    gt.second("f")
    gt.share(0)
    g1.forward("l")
    preconds(True, 6, 8)
    g1.forward("o")
    g0.far_row()
    gt.shared(0)
    applied([(other, p1)])
    g1.forward("r")
    g0.all_shared()
    gt.forward("l")
    grad_piece(0)
    grad_piece(1)
    applied([(c, p2)])
    gt.forward("r")
    g1.forward("f")
    g1.near_row("l")
    g1.near_row("r")
    grad_piece(2)
    grad_piece(3)
    gt.forward("o")
    gt.forward("f")
    gt.near_row("l")
    applied([(c, left2)])
    gt.near_row("r")
    applied([(c, right2)])
    g1.far_row()
    gt.shared(3)
    applied([(other, left1)])
    gt.far_block("l")
    gt.shared(1)
    gt.far_block("o")
    applied_blocks(c, far2, (p1, left1))
    g1.all_shared()
    grad_piece(4)
    grad_piece(5)
    gt.far_block("f")
    gt.far_block("r")
    applied([(other, right1)])
    grad_piece(6)
    grad_piece(7)
    gt.shared_block("o")
    gt.shared_block("l")
    gt.shared_block("f")
    gt.shared_block("r")
    applied_blocks(other, far1, (right2, far2))
    applied_blocks(other, far1, (p2, left2))
    applied_blocks(c, far2, (right1, far1))

    sums = [jnp.zeros((8, TG), F32)] * Q
    for i in range(FL // 8):
        gr = gr_v[i * 8:(i + 1) * 8]
        for q in range(Q):
            sums[q] += acc_v[q * FL + i * 8:q * FL + (i + 1) * 8] * gr
    sc = jnp.concatenate([jnp.sum(v, axis=0, keepdims=True) for v in sums], axis=0)
    place1 = x * 2 + c
    red1[place1] = jnp.concatenate([sc[:, :128], sc[:, 128:]], axis=0)
    for k in range(1, 8):
        to = lax.rem(place1 + k, 8)
        send(f"s1{k}", red1.at[place1], red1.at[place1], {"eig": y * 8 + to})
    for cp in sent:
        cp.wait_send()
    sent.clear()
    for k in range(1, 8):
        recv(f"s1{k}", red1.at[lax.rem(place1 + 8 - k, 8)])
    red2[z, y] = jnp.sum(red1[...], axis=0)
    for kz in range(4):
        for ky in range(4):
            if kz or ky:
                send(f"s2{kz}{ky}", red2.at[z, y], red2.at[z, y],
                     {"grp": mod4(z + kz), "eig": mod4(y + ky) * 8 + place1})
    for cp in sent:
        cp.wait_send()
    for kz in range(4):
        for ky in range(4):
            if kz or ky:
                recv(f"s2{kz}{ky}", red2.at[mod4(z - kz), mod4(y - ky)])
    for g in range(GRP):
        total = jnp.sum(red2[g], axis=0)
        for half in range(2):
            out_ref[:, g * TG + half * 128:g * TG + (half + 1) * 128] = total[half * 4:half * 4 + 4]
    assert len(tags) <= NSEM, len(tags)


def per_device(out_grads, activations, grad_basis, act_basis, corrections, query_left, query_right):
    any_, vmem = pl.BlockSpec(memory_space=pl.ANY), pl.BlockSpec(memory_space=pltpu.VMEM)
    out = pl.pallas_call(
        body,
        out_shape=jax.ShapeDtypeStruct((Q, T), F32),
        in_specs=[any_] * 7,
        out_specs=vmem,
        scratch_shapes=[
            pltpu.VMEM((2, ROWS, KA), BF16),
            pltpu.VMEM((2, ROWS, KG), BF16),
            pltpu.VMEM((2, 4, 4, 16, KA), BF16),
            pltpu.VMEM((2, NG, 4, 4, 16, KC), BF16),
            pltpu.VMEM((2, 2, 4, 4, 2, R, DL), BF16),
            pltpu.VMEM((2, 4, 4, TG, DL), BF16),
            pltpu.VMEM((8, 4, QI, DL), BF16),
            pltpu.VMEM((2, FL, KB), BF16),
            pltpu.VMEM((4, KP, DL), BF16),
            pltpu.VMEM((Q, R, FL), BF16),
            pltpu.VMEM((2, QP, 2 * R), BF16),
            pltpu.VMEM((4, FL, DL), F32),
            pltpu.VMEM((2, TG, DL), F32),
            pltpu.VMEM((FL, TG), F32),
            pltpu.VMEM((QI, TG), F32),
            pltpu.VMEM((8, 8, 128), F32),
            pltpu.VMEM((GRP, 4, 8, 128), F32),
            pltpu.SemaphoreType.DMA((NSEM,)),
            pltpu.SemaphoreType.DMA((NSEM,)),
            pltpu.SemaphoreType.DMA((43,)),
        ],
        compiler_params=pltpu.CompilerParams(
            collective_id=0, has_side_effects=True, vmem_limit_bytes=60 * 1024 * 1024),
    )(activations, out_grads, grad_basis.T, act_basis, corrections, query_left, query_right)
    return out.T


def solution(mesh):
    placed = (
        P(("grp", "eig"), None),
        P(("grp", "eig"), None),
        P(None, "eig"),
        P(None, "eig"),
        P("eig", None),
        P(None, None, "eig"),
        P(None, None, "eig"),
    )
    return jax.shard_map(per_device, mesh=mesh, in_specs=placed, out_specs=P(), check_vma=False)
```

```python
import jax
import jax.numpy as jnp
from jax import lax
from jax.experimental import pallas as pl
from jax.experimental.pallas import tpu as pltpu
from jax.sharding import PartitionSpec as P

MESH = pl.DeviceIdType.MESH
F32, BF16 = jnp.float32, jnp.bfloat16

FF, D, Q, R, T = 14336, 8192, 4, 32, 1024
EIG, GRP = 32, 4
ROWS = T // (EIG * GRP)
TG = T // GRP
FL, DL = FF // EIG, D // EIG
KP = D // 8
KA = D // 2
KG = FF // 2
NG = 2
KC = KG // NG
KB = KC // 2
QI = Q * FL
QP = 2 * FL
NSEM = 120

NT = (((1,), (1,)), ((), ()))


def body(
    a_hbm, g_hbm, bt_hbm, ab_hbm, corr_hbm, ql_hbm, qr_hbm, out_ref,
    a_in, g_in, abuf, gbuf, rbuf, arbuf, pbuf, bt_v, ab_v, ql_v, lbd, inv_v,
    act_v, gr_v, acc_v, red1, red2, ssem, rsem, lsem,
):
    e = lax.axis_index("eig")
    z = lax.axis_index("grp")
    c, x, y = lax.rem(e, 2), lax.rem(e // 2, 4), e // 8
    s1, s2 = 2 + 6 * c, 8 - 6 * c
    p1, p2 = x + c * (y - x), y + c * (x - y)
    mod4 = lambda v: lax.rem(v + 4, 4)
    d1 = lambda k: {"eig": c + mod4(p1 + k) * s1 + p2 * s2}
    d2 = lambda k: {"eig": c + p1 * s1 + mod4(p2 + k) * s2}
    dz = lambda k: {"grp": mod4(z + k)}
    sib = {"eig": e + 1 - 2 * c}

    tags, sent = {}, []

    def send(tag, src, dst, dev):
        i = tags.setdefault(tag, len(tags))
        cp = pltpu.make_async_remote_copy(
            src_ref=src, dst_ref=dst, send_sem=ssem.at[i], recv_sem=rsem.at[i],
            device_id=dev, device_id_type=MESH)
        cp.start()
        sent.append(cp)

    def recv(tag, ref):
        pltpu.make_async_copy(ref, ref, rsem.at[tags[tag]]).wait()

    def local(i, src, dst):
        return pltpu.make_async_copy(src, dst, lsem.at[i])

    ld_a = local(0, a_hbm.at[:, pl.ds(pl.multiple_of(c * KA, KA), KA)], a_in.at[c])
    ld_g = local(1, g_hbm.at[:, pl.ds(pl.multiple_of(c * KG, KG), KG)], g_in.at[c])
    pair = lax.rem(z, 2)
    r_own = qr_hbm.at[pl.ds(2 * pair, 2)]
    ld_r = local(2, r_own, rbuf.at[c, pair, p2, p1])
    ld_ql = local(3, ql_hbm, ql_v)

    def ld_ab(cc, i):
        at = pl.multiple_of((cc * 4 + i) * KP, KP)
        return local(7 + i, ab_hbm.at[pl.ds(at, KP)], ab_v.at[i])

    def ld_bt(i):
        k, cc, h = i // 4, i // 2 % 2, i % 2
        return local(5 + i % 2, bt_hbm.at[:, pl.ds(cc * KG + k * KC + h * KB, KB)], bt_v.at[i % 2])

    def ld_corr(n, b):
        cc, row = n // 4, lax.rem(n, 4)
        eig = cc + b * (2 + 6 * cc) + row * (8 - 6 * cc)
        return local(11 + n * 4 + b, corr_hbm.at[:, pl.ds(pl.multiple_of(eig * DL, DL), DL)],
                     pbuf.at[n, b, pl.ds(pl.multiple_of((1 - pair) * QP, QP), FL)])

    for cp in (ld_a, ld_g, ld_r, ld_ql):
        cp.start()
    def large_loads():
        def corr(n, _):
            for b in range(4):
                ld_corr(n, b).start()
            return 0

        for i in range(4):
            ld_ab(c, i).start()
        lax.fori_loop(0, 8, corr, 0)
        for i in range(2):
            ld_bt(i).start()

    barrier = pltpu.get_barrier_semaphore()
    for dev in (d1(1), d1(2), d1(3), d2(1), d2(3), dz(1), dz(3), sib):
        pl.semaphore_signal(barrier, inc=1, device_id=dev, device_id_type=MESH)
    pl.semaphore_wait(barrier, 8)

    left1, right1, far1 = mod4(p1 + 3), mod4(p1 + 1), mod4(p1 + 2)
    left2, right2, far2 = mod4(p2 + 3), mod4(p2 + 1), mod4(p2 + 2)
    place = {"o": p1, "l": left1, "r": right1, "f": far1}
    place2 = {"o": p2, "l": left2, "r": right2, "f": far2}

    class Gather:
        def __init__(self, nm, blk, half):
            self.nm, self.blk, self.half = nm, blk, half

        def _send(self, tag, ref, dev):
            send(self.nm + tag, ref, ref, dev)

        def first(self):
            own = self.blk(p2, p1)
            self._send("1+", own, d1(1))
            self._send("1-", own, d1(3))

        def first_forward(self, b):
            if b == "l":
                recv(self.nm + "1+", self.blk(p2, left1))
                self._send("1f+", self.half(left1, 0), d1(1))
            else:
                recv(self.nm + "1-", self.blk(p2, right1))
                self._send("1f-", self.half(right1, 1), d1(3))

        def first_far(self):
            recv(self.nm + "1f+", self.half(far1, 0))
            recv(self.nm + "1f-", self.half(far1, 1))

        def second(self, b):
            ref = self.blk(p2, place[b])
            self._send("2+" + b, ref, d2(1))
            self._send("2-" + b, ref, d2(3))

        def forward(self, b):
            if b in "of":
                recv(self.nm + "2+" + b, self.blk(left2, place[b]))
                self._send("2f" + b, self.blk(left2, place[b]), d2(1))
            else:
                recv(self.nm + "2-" + b, self.blk(right2, place[b]))
                self._send("2f" + b, self.blk(right2, place[b]), d2(3))

        def share(self, k):
            self._send(f"s{k}", self.row(c, mod4(p2 + k)), sib)

        def near_row(self, b):
            if b == "l":
                recv(self.nm + "2+l", self.blk(left2, left1))
                recv(self.nm + "2+r", self.blk(left2, right1))
                self.share(3)
            else:
                recv(self.nm + "2-o", self.blk(right2, p1))
                recv(self.nm + "2-f", self.blk(right2, far1))
                self.share(1)

        def far_row(self):
            for b in "olrf":
                recv(self.nm + "2f" + b, self.blk(far2, place[b]))
            self.share(2)

        def far_block(self, b):
            ref = self.blk(far2, place[b])
            recv(self.nm + "2f" + b, ref)
            self._send("s2" + b, ref, sib)

        def shared_block(self, b):
            recv(self.nm + "s2" + b, self.blk(far1, place2[b], other))

        def shared(self, k):
            recv(f"{self.nm}s{k}", self.row(other, mod4(p1 + k)))

        def all_shared(self):
            for k in range(4):
                self.shared(k)

    other = 1 - c
    ga = Gather("a", lambda row, at: abuf.at[c, row, at],
                lambda at, h: abuf.at[c, p2, at, :, pl.ds(h * (KA // 2), KA // 2)])
    ga.row = lambda cc, row: abuf.at[cc, row]

    def gather_g(k):
        g = Gather(f"g{k}", lambda row, at: gbuf.at[c, k, row, at],
                   lambda at, h: gbuf.at[c, k, p2, at, :, pl.ds(h * (KC // 2), KC // 2)])
        g.row = lambda cc, row: gbuf.at[cc, k, row]
        return g

    g0, g1 = gather_g(0), gather_g(1)
    gt = Gather("t", lambda row, at, cc=c: arbuf.at[cc, row, at],
                 lambda at, h: arbuf.at[c, p2, at, pl.ds(h * (TG // 2), TG // 2)])
    gt.row = lambda cc, row: arbuf.at[cc, row]

    def act_half(cc, more):
        total = None
        for i in range(4):
            ld_ab(0, i).wait()
            av = abuf[cc, :, :, :, i * KP:(i + 1) * KP].reshape(TG, KP)
            part = jnp.dot(av, ab_v[i], preferred_element_type=F32)
            total = part if i == 0 else total + part
            if more:
                ld_ab(other, i).start()
        act_v[cc] = total

    def act_rot_own():
        act_half(c, True)

    def act_rot_other():
        ga.all_shared()
        act_half(other, False)
        turned = jnp.swapaxes(act_v[1].reshape(4, 4, 16, DL), 0, 1).reshape(TG, DL)
        arbuf[c, p2, p1] = (act_v[0] + turned).astype(BF16)

    def precond(second, n):
        at = 1 - pair if second else pair
        cc, row = n // 4, lax.rem(n, 4)
        if not second:
            for b in range(4):
                ld_corr(n, b).wait()

        for b in range(4):
            corr = pbuf[n, b, pl.ds(pl.multiple_of((1 - pair) * QP, QP), FL)]
            inv_v[b] = 1.0 / (corr.astype(F32) + 0.1)
        right = jnp.concatenate([rbuf[cc, at, row, b].reshape(2 * R, DL) for b in range(4)], axis=1)
        for q in range(2):
            prod = jnp.dot(lbd[at, q * FL:(q + 1) * FL], right, preferred_element_type=F32)
            for b in range(4):
                pbuf[n, b, pl.ds(pl.multiple_of(at * QP + q * FL, FL), FL)] = (
                    prod[:, b * DL:(b + 1) * DL] * inv_v[b]).astype(BF16)

    def preconds(second, lo, hi):
        for n in range(lo, hi):
            precond(second, n)

    def grad_piece(i):
        k, cc, h = i // 4, i // 2 % 2, i % 2
        ld_bt(i).wait()
        gv = gbuf[cc, k, :, :, :, h * KB:(h + 1) * KB]
        if cc == 1:
            gv = jnp.swapaxes(gv, 0, 1)
        part = lax.dot_general(bt_v[i % 2], gv.reshape(TG, KB), NT, preferred_element_type=F32)
        if i == 0:
            gr_v[...] = part
        else:
            gr_v[...] += part
        if i + 2 < 8:
            ld_bt(i + 2).start()

    def applied(groups):
        for cc, row in groups:
            applied_blocks(cc, row, range(4))

    def applied_blocks(cc, row, ats):
        rhs = jnp.concatenate([arbuf[cc, row, at] for at in ats], axis=1)
        for m in range(7):
            rows = slice(m * 256, (m + 1) * 256)
            lhs = jnp.concatenate([pbuf[cc * 4 + row, at, rows] for at in ats], axis=1)
            acc_v[rows] += lax.dot_general(lhs, rhs, NT, preferred_element_type=F32)

    def share_pair(k):
        ref = rbuf.at[c, 1 - pair, :, :, k // 2]
        recv(f"rz{k}", ref)
        send(f"rs{k}", ref, ref, sib)

    def left_factors():
        ld_ql.wait()
        for at in range(2):
            lt = ql_v[2 * at:2 * at + 2].reshape(2 * R, FL).astype(F32)
            lt = jnp.concatenate([lt, jnp.zeros((2 * R, 512 - FL), F32)], axis=1)
            lt = jnp.concatenate([lt, jnp.zeros((2 * R, 512), F32)], axis=0).T[:FL]
            lane = lax.broadcasted_iota(jnp.int32, (FL, 4 * R), 1)
            for q in range(2):
                keep = (lane >= q * R) & (lane < (q + 1) * R)
                lbd[at, q * FL:(q + 1) * FL] = jnp.where(keep, lt, 0.0)[:, :2 * R].astype(BF16)

        acc_v[...] = jnp.zeros_like(acc_v)

    def own_activations():
        ld_a.wait()
        recv("sa", a_in.at[other])
        abuf[c, p2, p1] = jnp.concatenate([a_in[0].astype(F32), a_in[1].astype(F32)], axis=0).astype(BF16)

    def own_out_grads():
        ld_g.wait()
        recv("sg", g_in.at[other])
        for k in range(NG):
            cols = slice(k * KC, (k + 1) * KC)
            gbuf[c, k, p2, p1] = jnp.concatenate(
                [g_in[0, :, cols].astype(F32), g_in[1, :, cols].astype(F32)], axis=0).astype(BF16)

    def right_rows():
        ld_r.wait()
        for k in (1, 3, 2):
            recv(f"r1{k}", rbuf.at[c, pair, p2, mod4(p1 - k)])
        for k, dev in (("+", d2(1)), ("-", d2(3))):
            send("r2" + k, rbuf.at[c, pair, p2], rbuf.at[c, pair, p2], dev)

    def right_half(row, h):
        return rbuf.at[c, pair, row, pl.ds(2 * h, 2)]

    def right_forward():
        recv("r2+", rbuf.at[c, pair, left2])
        send("r2f+", right_half(left2, 0), right_half(left2, 0), d2(1))
        recv("r2-", rbuf.at[c, pair, right2])
        send("r2f-", right_half(right2, 1), right_half(right2, 1), d2(3))

    def right_along_z():
        recv("r2f+", right_half(far2, 0))
        recv("r2f-", right_half(far2, 1))
        for k in (1, 3):
            ref = rbuf.at[c, pair, :, :, k // 2]
            send(f"rz{k}", ref, ref, dz(k))
        send("rs0", rbuf.at[c, pair], rbuf.at[c, pair], sib)

    send("sa", a_hbm.at[:, pl.ds(pl.multiple_of(other * KA, KA), KA)], a_in.at[c], sib)
    for k in (1, 3, 2):
        send(f"r1{k}", r_own, rbuf.at[c, pair, p2, p1], d1(k))
    send("sg", g_hbm.at[:, pl.ds(pl.multiple_of(other * KG, KG), KG)], g_in.at[c], sib)
    own_activations()
    ga.first()
    own_out_grads()
    g0.first()
    right_rows()
    ga.first_forward("r")
    ga.second("o")
    large_loads()
    ga.second("r")
    ga.first_forward("l")
    ga.second("l")
    ga.first_far()
    ga.second("f")
    left_factors()
    right_forward()
    g0.first_forward("l")
    g0.first_forward("r")
    ga.forward("l")
    ga.forward("o")
    g1.first()
    ga.forward("r")
    ga.near_row("r")
    ga.forward("f")
    g0.second("l")
    g0.second("r")
    ga.share(0)
    right_along_z()
    recv("rs0", rbuf.at[other, pair])
    g0.second("o")
    preconds(False, 0, 2)
    ga.near_row("l")
    ga.far_row()
    g0.first_far()
    g0.second("f")
    preconds(False, 2, 4)
    g1.first_forward("l")
    g1.second("l")
    g1.first_forward("r")
    g1.second("r")
    act_rot_own()
    act_rot_other()
    gt.first()
    preconds(False, 4, 6)
    share_pair(3)
    g0.forward("f")
    share_pair(1)
    g1.second("o")
    g0.forward("r")
    preconds(False, 6, 8)
    g0.forward("o")
    g1.first_far()
    g0.forward("l")
    g1.share(0)
    g0.near_row("r")
    gt.second("o")
    gt.first_forward("r")
    gt.first_forward("l")
    for k in (1, 3):
        recv(f"rs{k}", rbuf.at[other, 1 - pair, :, :, k // 2])
    preconds(True, 0, 2)
    g0.share(0)
    gt.second("l")
    preconds(True, 2, 4)
    g0.near_row("l")
    preconds(True, 4, 6)
    gt.second("r")
    g1.second("f")
    gt.first_far()
    gt.second("f")
    gt.share(0)
    g1.forward("l")
    preconds(True, 6, 8)
    g1.forward("o")
    g0.far_row()
    gt.shared(0)
    applied([(other, p1)])
    g1.forward("r")
    g0.all_shared()
    gt.forward("l")
    grad_piece(0)
    grad_piece(1)
    applied([(c, p2)])
    gt.forward("r")
    g1.forward("f")
    g1.near_row("l")
    g1.near_row("r")
    grad_piece(2)
    grad_piece(3)
    gt.forward("o")
    gt.forward("f")
    gt.near_row("l")
    applied([(c, left2)])
    gt.near_row("r")
    applied([(c, right2)])
    g1.far_row()
    gt.shared(3)
    applied([(other, left1)])
    gt.far_block("l")
    gt.shared(1)
    gt.far_block("o")
    applied_blocks(c, far2, (p1, left1))
    g1.all_shared()
    grad_piece(4)
    grad_piece(5)
    gt.far_block("f")
    gt.far_block("r")
    applied([(other, right1)])
    grad_piece(6)
    grad_piece(7)
    gt.shared_block("o")
    gt.shared_block("l")
    gt.shared_block("f")
    gt.shared_block("r")
    applied_blocks(other, far1, (right2, far2))
    applied_blocks(other, far1, (p2, left2))
    applied_blocks(c, far2, (right1, far1))

    sums = [jnp.zeros((8, TG), F32)] * Q
    for i in range(FL // 8):
        gr = gr_v[i * 8:(i + 1) * 8]
        for q in range(Q):
            sums[q] += acc_v[q * FL + i * 8:q * FL + (i + 1) * 8] * gr
    sc = jnp.concatenate([jnp.sum(v, axis=0, keepdims=True) for v in sums], axis=0)
    place1 = x * 2 + c
    red1[place1] = jnp.concatenate([sc[:, :128], sc[:, 128:]], axis=0)
    for k in (4, 5, 3, 6, 2, 1, 7):
        to = lax.rem(place1 + k, 8)
        send(f"s1{k}", red1.at[place1], red1.at[place1], {"eig": y * 8 + to})
    for cp in sent:
        cp.wait_send()
    sent.clear()
    for k in range(1, 8):
        recv(f"s1{k}", red1.at[lax.rem(place1 + 8 - k, 8)])
    red2[z, y] = jnp.sum(red1[...], axis=0)
    for kz in (2, 1, 3, 0):
        for ky in (2, 1, 3, 0):
            if kz or ky:
                send(f"s2{kz}{ky}", red2.at[z, y], red2.at[z, y],
                     {"grp": mod4(z + kz), "eig": mod4(y + ky) * 8 + place1})
    for cp in sent:
        cp.wait_send()
    for kz in range(4):
        for ky in range(4):
            if kz or ky:
                recv(f"s2{kz}{ky}", red2.at[mod4(z - kz), mod4(y - ky)])
    for g in range(GRP):
        total = jnp.sum(red2[g], axis=0)
        for half in range(2):
            out_ref[:, g * TG + half * 128:g * TG + (half + 1) * 128] = total[half * 4:half * 4 + 4]
    assert len(tags) <= NSEM, len(tags)


def per_device(out_grads, activations, grad_basis, act_basis, corrections, query_left, query_right):
    any_, vmem = pl.BlockSpec(memory_space=pl.ANY), pl.BlockSpec(memory_space=pltpu.VMEM)
    out = pl.pallas_call(
        body,
        out_shape=jax.ShapeDtypeStruct((Q, T), F32),
        in_specs=[any_] * 7,
        out_specs=vmem,
        scratch_shapes=[
            pltpu.VMEM((2, ROWS, KA), BF16),
            pltpu.VMEM((2, ROWS, KG), BF16),
            pltpu.VMEM((2, 4, 4, 16, KA), BF16),
            pltpu.VMEM((2, NG, 4, 4, 16, KC), BF16),
            pltpu.VMEM((2, 2, 4, 4, 2, R, DL), BF16),
            pltpu.VMEM((2, 4, 4, TG, DL), BF16),
            pltpu.VMEM((8, 4, QI, DL), BF16),
            pltpu.VMEM((2, FL, KB), BF16),
            pltpu.VMEM((4, KP, DL), BF16),
            pltpu.VMEM((Q, R, FL), BF16),
            pltpu.VMEM((2, QP, 2 * R), BF16),
            pltpu.VMEM((4, FL, DL), F32),
            pltpu.VMEM((2, TG, DL), F32),
            pltpu.VMEM((FL, TG), F32),
            pltpu.VMEM((QI, TG), F32),
            pltpu.VMEM((8, 8, 128), F32),
            pltpu.VMEM((GRP, 4, 8, 128), F32),
            pltpu.SemaphoreType.DMA((NSEM,)),
            pltpu.SemaphoreType.DMA((NSEM,)),
            pltpu.SemaphoreType.DMA((43,)),
        ],
        compiler_params=pltpu.CompilerParams(
            collective_id=0, has_side_effects=True, vmem_limit_bytes=60 * 1024 * 1024),
    )(activations, out_grads, grad_basis.T, act_basis, corrections, query_left, query_right)
    return out.T


def solution(mesh):
    placed = (
        P(("grp", "eig"), None),
        P(("grp", "eig"), None),
        P(None, "eig"),
        P(None, "eig"),
        P("eig", None),
        P(None, None, "eig"),
        P(None, None, "eig"),
    )
    return jax.shard_map(per_device, mesh=mesh, in_specs=placed, out_specs=P(), check_vma=False)
```
